32 devices in a mesh: ctx: 8 (over z, x), grp: 4 (over y, core).
Axes of the slice: x: 2, y: 2, z: 4, core: 2. Of those that a mesh axis runs over, the one named last changes fastest.
Arguments:
- queries: bfloat16 [5120, 4096], P(('ctx', 'grp')), may hold values from -27 to 27
- keys: bfloat16 [5120, 512], P(('ctx', 'grp')), may hold values from -4.5 to 4.5
- values: bfloat16 [5120, 512], P(('ctx', 'grp')), may hold values from -6 to 6
- lengths: int32 [16], replicated, may hold values from 1 to 640, 5120 in all
- ssmax_scale: float32 [32], replicated, may hold values from 0.3 to 0.9
Outputs:
- attended: bfloat16 [5120, 4096], P(('ctx', 'grp'))
The draws below stay inside these ranges and needn't reach their ends.
Inputs may be any that keep to these rules, and one draw needn't show every extreme that they name: Every document has 1 to 640 tokens and one has exactly 640; the lengths sum to 5120.
All inputs are finite; a program needn't handle non-finite values.
Results may differ from the reference program's by a relative error of at most 0.0047.
Values may be sent and summed in bfloat16 or wider, within the bound.
A program may use at most 64 MiB of HBM per device.

```python
import math
import jax
import jax.numpy as jnp
import numpy as np
from jax import lax

HQ = 32
HK = 4
HD = 128
TOK_DEV = 160
WIN_DEV = 4
MOST = 640
TOKENS = 5120
NDOC = 16


def joint_rows(key):
    return jnp.clip(jax.random.normal(jax.random.fold_in(key, 101), (TOKENS, HK, HD), jnp.float32), -4.0, 4.0)


def draw_keys(key, part):
    base = joint_rows(key)
    return base.reshape(TOKENS, HK * HD).astype(jnp.bfloat16)


def draw_queries(key, part):
    drawn = jnp.clip(jax.random.normal(jax.random.fold_in(key, 303), (TOKENS, HQ, HD), jnp.float32), -4.0, 4.0)
    return drawn.reshape(TOKENS, HQ * HD).astype(jnp.bfloat16)


def steps_of(stream_key, dims, cuts, low, largest):
    loudness = 1.0
    for axis_at, shards_of in cuts:
        draws = jax.random.uniform(jax.random.fold_in(jax.random.fold_in(stream_key, 6), axis_at), (shards_of,), jnp.float32, low / len(cuts), largest / len(cuts))
        loudness = loudness * jnp.repeat(jnp.exp(draws), dims[axis_at] // shards_of).reshape((-1,) + (1,) * (len(dims) - 1 - axis_at))
    return loudness


def split_up(count, total, limit, skew):
    portions = [(1 << 20) // math.isqrt(rank ** skew) + 1 for rank in range(2, count + 1)]
    spare, given = total - limit - (count - 1), [1] * (count - 1)
    while spare > 0:
        candidates = [i for i in range(count - 1) if given[i] < limit]
        whole, left = sum([portions[i] for i in candidates]), spare
        for i in candidates:
            extra = min(limit - given[i], max(1, left * portions[i] // whole), spare)
            given[i] = given[i] + extra
            spare = spare - extra
    return np.array([limit] + given)


def ragged(rng, number_of, total, bound, slope):
    if number_of == 2:
        one = jax.random.randint(rng, (), max(1, total - bound), min(bound, total - 1) + 1)
        return jnp.stack([one, total - one])
    tallies = jnp.asarray(split_up(number_of, total, bound, slope), jnp.int32)
    couples = (number_of - 1) // 2
    source_of, sink = tallies[1:1 + 2 * couples:2], tallies[2:2 + 2 * couples:2]
    margin = jnp.minimum(source_of - 1, bound - sink)
    passed = jax.random.randint(jax.random.fold_in(rng, 1), (couples,), 0, 1 << 20) % (margin + 1)
    tallies = tallies.at[1:1 + 2 * couples:2].set(source_of - passed).at[2:2 + 2 * couples:2].set(sink + passed)
    return tallies[jax.random.permutation(jax.random.fold_in(rng, 2), number_of)]


def bell_draw(rng, dims, spread, reach, cuts=(), held_as=jnp.bfloat16):
    gain = steps_of(rng, dims, cuts, -0.22, 0.18) if cuts else 1.0
    values = jax.random.normal(rng, dims, jnp.float32) * spread * gain
    return jnp.minimum(jnp.maximum(values, -reach), reach).astype(held_as)


def setup_inputs(seed: int = 0) -> dict:
    arg_keys = jax.random.split(jax.random.key(seed), 6)
    queries = draw_queries(jax.random.fold_in(arg_keys[5], 71), 0)
    keys = draw_keys(jax.random.fold_in(arg_keys[5], 71), 0)
    values = bell_draw(arg_keys[2], (TOKENS, HK * HD), 1.0, 6.0, ((0, 32),))
    lengths = ragged(arg_keys[3], NDOC, TOKENS, MOST, 2).astype(jnp.int32)
    ssmax_scale = jnp.clip(jnp.exp(jax.random.uniform(arg_keys[4], (HQ,), jnp.float32, math.log(0.3), math.log(0.9))), 0.3, 0.9)
    return {"queries": queries, "keys": keys, "values": values, "lengths": lengths, "ssmax_scale": ssmax_scale}


def attend_rows(q_rows, k_window, v_window, q_pos, k_pos, lengths, ssmax_scale):
    rows = q_rows.shape[0]
    win_width = k_window.shape[0]
    per_group = HQ // HK
    totals = jnp.cumsum(lengths, dtype=jnp.int32)
    before = totals[None, :] <= q_pos[:, None]
    doc_start = lax.optimization_barrier(jnp.sum(jnp.where(before, lengths[None, :], 0), axis=1, dtype=jnp.int32))
    visible = (q_pos - doc_start + 1).astype(jnp.float32)
    score_coef = ssmax_scale[None, :] * jnp.log(visible)[:, None] / jnp.sqrt(jnp.float32(HD))
    coef_heads = score_coef.reshape(rows, HK, per_group).transpose(1, 2, 0)[..., None]
    q_heads = q_rows.astype(jnp.float32).reshape(rows, HK, per_group, HD)
    k_heads = k_window.astype(jnp.float32).reshape(win_width, HK, HD)
    v_heads = v_window.astype(jnp.float32).reshape(win_width, HK, HD)
    scores = jnp.einsum('ikgd,jkd->kgij', q_heads, k_heads) * coef_heads
    live_mask = (k_pos[None, :] >= doc_start[:, None]) & (k_pos[None, :] <= q_pos[:, None])
    scores = jnp.where(live_mask[None, None], scores, -jnp.inf)
    top_score = lax.optimization_barrier(jnp.max(scores, axis=-1, keepdims=True))
    probs = jnp.exp(scores - top_score)
    weights = (probs / lax.optimization_barrier(jnp.sum(probs, axis=-1, keepdims=True))).astype(jnp.bfloat16)
    weights = lax.optimization_barrier(weights).astype(jnp.float32)
    mixed = jnp.einsum('kgij,jkd->ikgd', weights, v_heads)
    return mixed.reshape(rows, HQ * HD).astype(jnp.bfloat16)

def reference(queries, keys, values, lengths, ssmax_scale):
    doc_most = WIN_DEV * TOK_DEV
    blocks = TOKENS // TOK_DEV
    pad_keys = jnp.concatenate([jnp.zeros((doc_most, HK * HD), keys.dtype), keys], axis=0)
    pad_values = jnp.concatenate([jnp.zeros((doc_most, HK * HD), values.dtype), values], axis=0)

    def one_block(block_id):
        row_start = (block_id * TOK_DEV).astype(jnp.int32)
        q_rows = lax.dynamic_slice_in_dim(queries, row_start, TOK_DEV, 0)
        k_window = lax.dynamic_slice_in_dim(pad_keys, row_start, doc_most + TOK_DEV, 0)
        v_window = lax.dynamic_slice_in_dim(pad_values, row_start, doc_most + TOK_DEV, 0)
        q_pos = row_start + jnp.arange(TOK_DEV, dtype=jnp.int32)
        k_pos = row_start - doc_most + jnp.arange(doc_most + TOK_DEV, dtype=jnp.int32)
        return attend_rows(q_rows, k_window, v_window, q_pos, k_pos, lengths, ssmax_scale)
    outputs = lax.map(one_block, jnp.arange(blocks, dtype=jnp.int32))
    return outputs.reshape(TOKENS, HQ * HD)
```

```python
import functools
import math

import jax
import jax.numpy as jnp
from jax import lax
from jax.experimental import pallas as pl
from jax.experimental.pallas import tpu as pltpu
from jax.sharding import PartitionSpec as P

HQ = 32
HK = 4
HD = 128
WIN_DEV = 4
PER = HQ // HK
HALVES = 2
HALF = HK * HD // HALVES
MESH = pl.DeviceIdType.MESH
MASKED = -1e30


def kernel(
    n_ctx, n_grp, scale_ref, len_ref, q_ref, k_ref, v_ref, o_ref,
    kw, vw, bias_own, bias_win, lv, acc, top, send_sem, recv_sem,
):
    rows = q_ref.shape[0]
    n_dev = n_ctx * n_grp
    c = lax.axis_index("ctx")
    g = lax.axis_index("grp")
    me = c * n_grp + g
    core = lax.rem(g, 2)
    relay = n_grp == 4

    def at(lin):
        return (lin // n_grp, lin % n_grp)

    sibling = (c, g + 1 - 2 * core)
    across = (c, lax.rem(g + 2, 4))

    barrier = pltpu.get_barrier_semaphore()

    def greet(dev):
        pl.semaphore_signal(barrier, inc=1, device_id=dev, device_id_type=MESH)

    has4, to4 = me >= 4, me + 4 < n_dev
    has2, to2 = me >= 2, me + 2 < n_dev
    greet(sibling)
    count = 1 + has4.astype(jnp.int32) + to4.astype(jnp.int32)

    @pl.when(has4)
    def _():
        greet(at(me - 4))

    @pl.when(to4)
    def _():
        greet(at(me + 4))

    if relay:
        greet(across)
        count = count + 1
    else:
        count = count + has2.astype(jnp.int32) + to2.astype(jnp.int32)

        @pl.when(has2)
        def _():
            greet(at(me - 2))

        @pl.when(to2)
        def _():
            greet(at(me + 2))

    @pl.when(jnp.logical_not(has4))
    def _():
        kw[0] = jnp.zeros(kw.shape[1:], kw.dtype)
        vw[0] = jnp.zeros(vw.shape[1:], vw.dtype)

    if not relay:

        @pl.when(jnp.logical_not(has2))
        def _():
            kw[2] = jnp.zeros(kw.shape[1:], kw.dtype)
            vw[2] = jnp.zeros(vw.shape[1:], vw.dtype)

    pl.semaphore_wait(barrier, count)

    def copies(src_slot, dst_slot, kind, half, dev):
        cols = pl.ds(half * HALF, HALF)
        made = []
        for i, (own, win) in enumerate(((k_ref, kw), (v_ref, vw))):
            src = own.at[:, cols] if src_slot is None else win.at[src_slot, :, cols]
            made.append(
                pltpu.make_async_remote_copy(
                    src_ref=src,
                    dst_ref=win.at[dst_slot, :, cols],
                    send_sem=send_sem.at[kind, half, i],
                    recv_sem=recv_sem.at[dst_slot, half, i],
                    device_id=dev,
                    device_id_type=MESH,
                )
            )
        return made

    def start(*args):
        for copy in copies(*args):
            copy.start()

    def arrived(slot, half):
        for copy in copies(None, slot, 0, half, sibling):
            copy.wait_recv()

    def sent(kind, half):
        for copy in copies(None, 0, kind, half, sibling):
            copy.wait_send()

    first_chip = g < 2
    for half in range(HALVES):

        @pl.when(to4)
        def _(half=half):
            start(None, 0, 0, half, at(me + 4))

        if relay:

            @pl.when(first_chip)
            def _(half=half):
                start(None, 2, 1, half, across)

        else:

            @pl.when(to2)
            def _(half=half):
                start(None, 2, 1, half, at(me + 2))

        @pl.when(core == 0)
        def _(half=half):
            start(None, 3, 2, half, sibling)

    def pass_on_far(half):
        @pl.when(has4)
        def _():
            arrived(0, half)

        if relay:

            @pl.when(jnp.logical_not(first_chip))
            def _():
                start(0, 2, 1, half, across)

        @pl.when(core == 1)
        def _():
            start(0, 1, 2, half, sibling)

    def pass_on_near(half):
        if relay:
            arrived(2, half)
        else:

            @pl.when(has2)
            def _():
                arrived(2, half)

        @pl.when(core == 0)
        def _():
            start(2, 1, 3, half, sibling)

        @pl.when(core == 1)
        def _():
            start(2, 3, 3, half, sibling)

    pos = me * rows + lax.broadcasted_iota(jnp.int32, (rows, HD), 0)

    def doc(j, carry):
        total, begin = carry
        total = total + len_ref[j]
        return total, jnp.where(total <= pos, total, begin)

    _, begin = lax.fori_loop(0, len_ref.shape[0], doc, (jnp.int32(0), jnp.zeros_like(pos)))
    visible = pos - begin + 1
    factor = jnp.log(visible.astype(jnp.float32)) * (math.log2(math.e) / math.sqrt(HD))
    lv[...] = jnp.where(visible == 1, 1.0, factor)
    for ref, base in ((bias_own, me * rows), (bias_win, (me - WIN_DEV) * rows)):
        shape = ref.shape
        k_pos = base + lax.broadcasted_iota(jnp.int32, shape, 1)
        q_pos = me * rows + lax.broadcasted_iota(jnp.int32, shape, 0)
        live = (k_pos >= jnp.broadcast_to(begin[:, :1], shape)) & (k_pos <= q_pos)
        ref[...] = jnp.where(live, 0.0, MASKED)

    def head_cols(h):
        return pl.ds(pl.multiple_of(h * HD, HD), HD)

    def stacked(kv):
        q = jnp.concatenate([q_ref[:, head_cols(kv * PER + i)] for i in range(PER)], axis=0)
        fac = jnp.concatenate([lv[...] * scale_ref[kv * PER + i] for i in range(PER)], axis=0)
        return q, fac[:, :1]

    def scores(q, keys, bias):
        s = lax.dot_general(q, keys, (((1,), (1,)), ((), ())), preferred_element_type=jnp.float32)
        s = s.reshape(PER, rows, bias.shape[1]) + bias[...][None]
        return s.reshape(PER * rows, bias.shape[1])

    def mix(p, vals):
        wide = jnp.concatenate([vals, jnp.ones(vals.shape, vals.dtype)], axis=1)
        return jnp.dot(p.astype(jnp.bfloat16), wide, preferred_element_type=jnp.float32)

    def own_part(kv, _):
        q, fac = stacked(kv)
        s = scores(q, k_ref[:, head_cols(kv)], bias_own)
        m = jnp.max(s, axis=1, keepdims=True)
        acc[kv] = mix(jnp.exp2((s - m) * fac), v_ref[:, head_cols(kv)])
        top[kv] = jnp.broadcast_to(m, top.shape[1:])
        return 0

    def window_part(kv, _):
        q, fac = stacked(kv)
        keys = kw[:, :, head_cols(kv)].reshape(WIN_DEV * rows, HD)
        vals = vw[:, :, head_cols(kv)].reshape(WIN_DEV * rows, HD)
        s = scores(q, keys, bias_win)
        m_own = top[kv][:, :1]
        m = jnp.maximum(m_own, jnp.max(s, axis=1, keepdims=True))
        part = mix(jnp.exp2((s - m) * fac), vals)
        both = acc[kv] * jnp.exp2((m_own - m) * fac) + part
        out = (both[:, :HD] / both[:, HD:]).astype(o_ref.dtype)
        for i in range(PER):
            o_ref[:, head_cols(kv * PER + i)] = out[i * rows : (i + 1) * rows]
        return 0

    per_half = HK // HALVES
    lax.fori_loop(0, per_half, own_part, 0)
    pass_on_far(0)
    lax.fori_loop(per_half, HK, own_part, 0)
    pass_on_near(0)
    pass_on_far(1)
    pass_on_near(1)
    for half in range(HALVES):
        arrived(1, half)
        arrived(3, half)
        lax.fori_loop(half * per_half, (half + 1) * per_half, window_part, 0)

    for half in range(HALVES):

        @pl.when(to4)
        def _(half=half):
            sent(0, half)

        if relay:
            sent(1, half)
        else:

            @pl.when(to2)
            def _(half=half):
                sent(1, half)

        sent(2, half)
        sent(3, half)


def body(queries, keys, values, lengths, ssmax_scale):
    rows = queries.shape[0]
    n_ctx, n_grp = lax.axis_size("ctx"), lax.axis_size("grp")
    vmem = pl.BlockSpec(memory_space=pltpu.VMEM)
    smem = pl.BlockSpec(memory_space=pltpu.SMEM)
    window = pltpu.VMEM((WIN_DEV, rows, HK * HD), jnp.bfloat16)
    pairs = HQ * rows * (WIN_DEV + 1) * rows
    return pl.pallas_call(
        functools.partial(kernel, n_ctx, n_grp),
        out_shape=jax.ShapeDtypeStruct(queries.shape, queries.dtype),
        in_specs=[smem, smem, vmem, vmem, vmem],
        out_specs=vmem,
        scratch_shapes=[
            window,
            window,
            pltpu.VMEM((rows, rows), jnp.float32),
            pltpu.VMEM((rows, WIN_DEV * rows), jnp.float32),
            pltpu.VMEM((rows, HD), jnp.float32),
            pltpu.VMEM((HK, PER * rows, 2 * HD), jnp.float32),
            pltpu.VMEM((HK, PER * rows, HD), jnp.float32),
            pltpu.SemaphoreType.DMA((4, HALVES, 2)),
            pltpu.SemaphoreType.DMA((4, HALVES, 2)),
        ],
        compiler_params=pltpu.CompilerParams(
            collective_id=0, has_side_effects=True, vmem_limit_bytes=48 * 1024 * 1024
        ),
        cost_estimate=pl.CostEstimate(
            flops=4 * pairs * HD, bytes_accessed=4 * queries.size, transcendentals=pairs
        ),
    )(ssmax_scale, lengths, queries, keys, values)


def solution(mesh):
    spec = P(("ctx", "grp"), None)
    return jax.shard_map(
        body,
        mesh=mesh,
        in_specs=(spec, spec, spec, P(), P()),
        out_specs=spec,
        check_vma=False,
    )
```

```python
import functools
import math

import jax
import jax.numpy as jnp
from jax import lax
from jax.experimental import pallas as pl
from jax.experimental.pallas import tpu as pltpu
from jax.sharding import PartitionSpec as P

HQ = 32
HK = 4
HD = 128
WIN_DEV = 4
PER = HQ // HK
HALVES = 2
HALF = HK * HD // HALVES
MESH = pl.DeviceIdType.MESH
MASKED = -1e30


def kernel(
    n_ctx, n_grp, scale_hbm, len_hbm, q_hbm, k_hbm, v_hbm, o_ref,
    scale_ref, len_ref, q_ref, k_ref, v_ref,
    kw, vw, bias, reach, live, lv, acc, top, load_sem, send_sem, recv_sem,
):
    rows = q_ref.shape[0]
    loads = [
        pltpu.make_async_copy(src, dst, load_sem.at[i])
        for i, (src, dst) in enumerate(
            (
                (len_hbm, len_ref),
                (scale_hbm, scale_ref),
                (k_hbm, k_ref),
                (v_hbm, v_ref),
                (q_hbm, q_ref),
            )
        )
    ]
    for copy in loads:
        copy.start()
    small, large = loads[:2], loads[2:]
    n_dev = n_ctx * n_grp
    c = lax.axis_index("ctx")
    g = lax.axis_index("grp")
    me = c * n_grp + g
    core = lax.rem(g, 2)
    relay = n_grp == 4

    def at(lin):
        return (lin // n_grp, lin % n_grp)

    sibling = (c, g + 1 - 2 * core)
    across = (c, lax.rem(g + 2, 4))

    barrier = pltpu.get_barrier_semaphore()

    def greet(dev):
        pl.semaphore_signal(barrier, inc=1, device_id=dev, device_id_type=MESH)

    has4, to4 = me >= 4, me + 4 < n_dev
    has2, to2 = me >= 2, me + 2 < n_dev
    greet(sibling)
    count = 1 + has4.astype(jnp.int32) + to4.astype(jnp.int32)

    @pl.when(has4)
    def _():
        greet(at(me - 4))

    @pl.when(to4)
    def _():
        greet(at(me + 4))

    if relay:
        greet(across)
        count = count + 1
    else:
        count = count + has2.astype(jnp.int32) + to2.astype(jnp.int32)

        @pl.when(has2)
        def _():
            greet(at(me - 2))

        @pl.when(to2)
        def _():
            greet(at(me + 2))

    @pl.when(jnp.logical_not(has4))
    def _():
        kw[0] = jnp.zeros(kw.shape[1:], kw.dtype)
        vw[0] = jnp.zeros(vw.shape[1:], vw.dtype)

    if not relay:

        @pl.when(jnp.logical_not(has2))
        def _():
            kw[2] = jnp.zeros(kw.shape[1:], kw.dtype)
            vw[2] = jnp.zeros(vw.shape[1:], vw.dtype)

    pl.semaphore_wait(barrier, count)

    def copies(src_slot, dst_slot, kind, half, dev):
        cols = pl.ds(half * HALF, HALF)
        made = []
        for i, (own, win) in enumerate(((k_hbm, kw), (v_hbm, vw))):
            src = own.at[:, cols] if src_slot is None else win.at[src_slot, :, cols]
            made.append(
                pltpu.make_async_remote_copy(
                    src_ref=src,
                    dst_ref=win.at[dst_slot, :, cols],
                    send_sem=send_sem.at[kind, half, i],
                    recv_sem=recv_sem.at[dst_slot, half, i],
                    device_id=dev,
                    device_id_type=MESH,
                )
            )
        return made

    def start(*args):
        for copy in copies(*args):
            copy.start()

    def arrived(slot, half):
        for copy in copies(None, slot, 0, half, sibling):
            copy.wait_recv()

    def sent(kind, half):
        for copy in copies(None, 0, kind, half, sibling):
            copy.wait_send()

    first_chip = g < 2
    for half in range(HALVES):

        @pl.when(to4)
        def _(half=half):
            start(None, 0, 0, half, at(me + 4))

        if relay:

            @pl.when(first_chip)
            def _(half=half):
                start(None, 2, 1, half, across)

        else:

            @pl.when(to2)
            def _(half=half):
                start(None, 2, 1, half, at(me + 2))

        @pl.when(core == 0)
        def _(half=half):
            start(None, 3, 2, half, sibling)

    def pass_on_far(half):
        @pl.when(has4)
        def _():
            arrived(0, half)

        if relay:

            @pl.when(jnp.logical_not(first_chip))
            def _():
                start(0, 2, 1, half, across)

        @pl.when(core == 1)
        def _():
            start(0, 1, 2, half, sibling)

    def pass_on_near(half):
        if relay:
            arrived(2, half)
        else:

            @pl.when(has2)
            def _():
                arrived(2, half)

        @pl.when(core == 0)
        def _():
            start(2, 1, 3, half, sibling)

        @pl.when(core == 1)
        def _():
            start(2, 3, 3, half, sibling)

    for copy in small:
        copy.wait()
    first = me * rows
    pos = first + lax.broadcasted_iota(jnp.int32, (rows, HD), 0)

    def doc(j, carry):
        total, begin = carry
        total = total + len_ref[j]
        return total, jnp.where(total <= pos, total, begin)

    _, begin = lax.fori_loop(0, len_ref.shape[0], doc, (jnp.int32(0), jnp.zeros_like(pos)))
    visible = pos - begin + 1
    factor = jnp.log(visible.astype(jnp.float32)) * (math.log2(math.e) / math.sqrt(HD))
    lv[...] = jnp.where(visible == 1, 1.0, factor)
    k_pos = first + lax.broadcasted_iota(jnp.int32, (rows, rows), 1)
    q_pos = first + lax.broadcasted_iota(jnp.int32, (rows, rows), 0)
    seen = (k_pos >= jnp.broadcast_to(begin[:, :1], (rows, rows))) & (k_pos <= q_pos)
    bias[...] = jnp.where(seen, 0.0, MASKED)
    reach[...] = jnp.where(begin < first, 1.0, 0.0)
    w_rows = WIN_DEV * rows
    w_pos = first - w_rows + lax.broadcasted_iota(jnp.int32, (w_rows, HD), 0)
    live[...] = jnp.where(w_pos >= begin[:1], 1.0, 0.0)
    for copy in large:
        copy.wait()

    def head_cols(h):
        return pl.ds(pl.multiple_of(h * HD, HD), HD)

    def scores(q, keys):
        return lax.dot_general(q, keys, (((1,), (1,)), ((), ())), preferred_element_type=jnp.float32)

    def spread(x, width):
        whole = [x] * (width // HD)
        if width % HD:
            whole.append(x[:, : width % HD])
        return jnp.concatenate(whole, axis=1)

    def mix(p, vals):
        return jnp.dot(p.astype(jnp.bfloat16), vals, preferred_element_type=jnp.float32)

    def own_part(kv, _):
        keys = k_ref[:, head_cols(kv)]
        vals = v_ref[:, head_cols(kv)]
        vals = jnp.concatenate([vals, jnp.ones(vals.shape, vals.dtype)], axis=1)
        for i in range(PER):
            h = kv * PER + i
            fac = spread(lv[...] * scale_ref[h], rows)
            s = scores(q_ref[:, head_cols(h)], keys) + bias[...]
            m = jnp.max(s, axis=1, keepdims=True)
            acc[h] = mix(jnp.exp2((s - m) * fac), vals)
            top[h] = jnp.broadcast_to(m, top.shape[1:])
        return 0

    def window_part(kv, _):
        alive = live[...]
        keys = kw[:, :, head_cols(kv)].reshape(w_rows, HD).astype(jnp.float32)
        keys = jnp.where(alive > 0, keys, k_ref[:16, head_cols(kv)].astype(jnp.float32)[:1])
        keys = keys.astype(jnp.bfloat16)
        vals = vw[:, :, head_cols(kv)].reshape(w_rows, HD).astype(jnp.float32)
        vals = jnp.concatenate([jnp.where(alive > 0, vals, 0.0), alive], axis=1).astype(jnp.bfloat16)
        reached = reach[...] > 0
        both_reached = spread(reach[...], 2 * HD) > 0
        for i in range(PER):
            h = kv * PER + i
            fac = lv[...] * scale_ref[h]
            s = scores(q_ref[:, head_cols(h)], keys)
            m_own = top[h]
            m_win = jnp.broadcast_to(jnp.max(s, axis=1, keepdims=True), m_own.shape)
            m = jnp.where(reached, jnp.maximum(m_own, m_win), m_own)
            part = mix(jnp.exp2((s - spread(m, w_rows)) * spread(fac, w_rows)), vals)
            kept = spread(jnp.exp2((m_own - m) * fac), 2 * HD)
            both = acc[h] * kept + jnp.where(both_reached, part, 0.0)
            o_ref[:, head_cols(h)] = (both[:, :HD] / both[:, HD:]).astype(o_ref.dtype)
        return 0

    per_half = HK // HALVES
    lax.fori_loop(0, 2, own_part, 0)
    pass_on_far(0)
    lax.fori_loop(2, 3, own_part, 0)
    pass_on_near(0)
    pass_on_far(1)
    lax.fori_loop(3, 4, own_part, 0)
    pass_on_near(1)
    for half in range(HALVES):
        arrived(1, half)
        arrived(3, half)
        lax.fori_loop(half * per_half, (half + 1) * per_half, window_part, 0)

    for half in range(HALVES):

        @pl.when(to4)
        def _(half=half):
            sent(0, half)

        if relay:
            sent(1, half)
        else:

            @pl.when(to2)
            def _(half=half):
                sent(1, half)

        sent(2, half)
        sent(3, half)


def body(queries, keys, values, lengths, ssmax_scale):
    rows = queries.shape[0]
    n_ctx, n_grp = lax.axis_size("ctx"), lax.axis_size("grp")
    vmem = pl.BlockSpec(memory_space=pltpu.VMEM)
    hbm = pl.BlockSpec(memory_space=pltpu.HBM)
    window = pltpu.VMEM((WIN_DEV, rows, HK * HD), jnp.bfloat16)
    pairs = HQ * rows * (WIN_DEV + 1) * rows
    return pl.pallas_call(
        functools.partial(kernel, n_ctx, n_grp),
        out_shape=jax.ShapeDtypeStruct(queries.shape, queries.dtype),
        in_specs=[hbm] * 5,
        out_specs=vmem,
        scratch_shapes=[
            pltpu.SMEM(ssmax_scale.shape, ssmax_scale.dtype),
            pltpu.SMEM(lengths.shape, lengths.dtype),
            pltpu.VMEM(queries.shape, queries.dtype),
            pltpu.VMEM(keys.shape, keys.dtype),
            pltpu.VMEM(values.shape, values.dtype),
            window,
            window,
            pltpu.VMEM((rows, rows), jnp.float32),
            pltpu.VMEM((rows, HD), jnp.float32),
            pltpu.VMEM((WIN_DEV * rows, HD), jnp.float32),
            pltpu.VMEM((rows, HD), jnp.float32),
            pltpu.VMEM((HQ, rows, 2 * HD), jnp.float32),
            pltpu.VMEM((HQ, rows, HD), jnp.float32),
            pltpu.SemaphoreType.DMA((5,)),
            pltpu.SemaphoreType.DMA((4, HALVES, 2)),
            pltpu.SemaphoreType.DMA((4, HALVES, 2)),
        ],
        compiler_params=pltpu.CompilerParams(
            collective_id=0, has_side_effects=True, vmem_limit_bytes=63 * 1024 * 1024
        ),
        cost_estimate=pl.CostEstimate(
            flops=4 * pairs * HD, bytes_accessed=4 * queries.size, transcendentals=pairs
        ),
    )(ssmax_scale, lengths, queries, keys, values)


def solution(mesh):
    spec = P(("ctx", "grp"), None)
    return jax.shard_map(
        body,
        mesh=mesh,
        in_specs=(spec, spec, spec, P(), P()),
        out_specs=spec,
        check_vma=False,
    )
```

```python
import functools
import math

import jax
import jax.numpy as jnp
from jax import lax
from jax.experimental import pallas as pl
from jax.experimental.pallas import tpu as pltpu
from jax.sharding import PartitionSpec as P

HQ = 32
HK = 4
HD = 128
WIN_DEV = 4
PER = HQ // HK
GROUP = 4
MESH = pl.DeviceIdType.MESH
MASKED = -1e30


def kernel(
    n_ctx, n_grp, scale_hbm, len_hbm, q_hbm, k_hbm, v_hbm, o_ref,
    scale_ref, len_ref, q_ref, k_ref, v_ref,
    kw, vw, bias, reach, live, lv, acc, top, load_sem, send_sem, recv_sem,
):
    rows = q_ref.shape[0]
    loads = [
        pltpu.make_async_copy(src, dst, load_sem.at[i])
        for i, (src, dst) in enumerate(
            (
                (len_hbm, len_ref),
                (scale_hbm, scale_ref),
                (k_hbm, k_ref),
                (v_hbm, v_ref),
                (q_hbm, q_ref),
            )
        )
    ]
    for copy in loads:
        copy.start()
    small, large = loads[:2], loads[2:]
    n_dev = n_ctx * n_grp
    c = lax.axis_index("ctx")
    g = lax.axis_index("grp")
    me = c * n_grp + g
    core = lax.rem(g, 2)
    relay = n_grp == 4

    def at(lin):
        return (lin // n_grp, lin % n_grp)

    sibling = (c, g + 1 - 2 * core)
    across = (c, lax.rem(g + 2, 4))

    barrier = pltpu.get_barrier_semaphore()

    def greet(dev):
        pl.semaphore_signal(barrier, inc=1, device_id=dev, device_id_type=MESH)

    has4, to4 = me >= 4, me + 4 < n_dev
    has2, to2 = me >= 2, me + 2 < n_dev
    greet(sibling)
    count = 1 + has4.astype(jnp.int32) + to4.astype(jnp.int32)

    @pl.when(has4)
    def _():
        greet(at(me - 4))

    @pl.when(to4)
    def _():
        greet(at(me + 4))

    if relay:
        greet(across)
        count = count + 1
    else:
        count = count + has2.astype(jnp.int32) + to2.astype(jnp.int32)

        @pl.when(has2)
        def _():
            greet(at(me - 2))

        @pl.when(to2)
        def _():
            greet(at(me + 2))

    @pl.when(jnp.logical_not(has4))
    def _():
        kw[0] = jnp.zeros(kw.shape[1:], kw.dtype)
        vw[0] = jnp.zeros(vw.shape[1:], vw.dtype)

    if not relay:

        @pl.when(jnp.logical_not(has2))
        def _():
            kw[2] = jnp.zeros(kw.shape[1:], kw.dtype)
            vw[2] = jnp.zeros(vw.shape[1:], vw.dtype)

    pl.semaphore_wait(barrier, count)

    def copies(src_slot, dst_slot, kind, part, dev):
        cols = pl.ds(part * HD, HD)
        made = []
        for i, (own, win) in enumerate(((k_hbm, kw), (v_hbm, vw))):
            src = own.at[:, cols] if src_slot is None else win.at[src_slot, :, cols]
            made.append(
                pltpu.make_async_remote_copy(
                    src_ref=src,
                    dst_ref=win.at[dst_slot, :, cols],
                    send_sem=send_sem.at[kind, part, i],
                    recv_sem=recv_sem.at[dst_slot, part, i],
                    device_id=dev,
                    device_id_type=MESH,
                )
            )
        return made

    def start(*args):
        for copy in copies(*args):
            copy.start()

    def arrived(slot, part):
        for copy in copies(None, slot, 0, part, sibling):
            copy.wait_recv()

    def sent(kind, part):
        for copy in copies(None, 0, kind, part, sibling):
            copy.wait_send()

    first_chip = g < 2
    for part in range(HK):

        @pl.when(to4)
        def _(part=part):
            start(None, 0, 0, part, at(me + 4))

        if relay:

            @pl.when(first_chip)
            def _(part=part):
                start(None, 2, 1, part, across)

        else:

            @pl.when(to2)
            def _(part=part):
                start(None, 2, 1, part, at(me + 2))

        @pl.when(core == 0)
        def _(part=part):
            start(None, 3, 2, part, sibling)

    def pass_on_far(part):
        @pl.when(has4)
        def _():
            arrived(0, part)

        if relay:

            @pl.when(jnp.logical_not(first_chip))
            def _():
                start(0, 2, 1, part, across)

        @pl.when(core == 1)
        def _():
            start(0, 1, 2, part, sibling)

    def pass_on_near(part):
        if relay:
            arrived(2, part)
        else:

            @pl.when(has2)
            def _():
                arrived(2, part)

        @pl.when(core == 0)
        def _():
            start(2, 1, 3, part, sibling)

        @pl.when(core == 1)
        def _():
            start(2, 3, 3, part, sibling)

    for copy in small:
        copy.wait()
    first = me * rows
    pos = first + lax.broadcasted_iota(jnp.int32, (rows, HD), 0)

    def doc(j, carry):
        total, begin = carry
        total = total + len_ref[j]
        return total, jnp.where(total <= pos, total, begin)

    _, begin = lax.fori_loop(0, len_ref.shape[0], doc, (jnp.int32(0), jnp.zeros_like(pos)))
    visible = pos - begin + 1
    factor = jnp.log(visible.astype(jnp.float32)) * (math.log2(math.e) / math.sqrt(HD))
    lv[...] = jnp.where(visible == 1, 1.0, factor)
    k_pos = first + lax.broadcasted_iota(jnp.int32, (rows, rows), 1)
    q_pos = first + lax.broadcasted_iota(jnp.int32, (rows, rows), 0)
    seen = (k_pos >= jnp.broadcast_to(begin[:, :1], (rows, rows))) & (k_pos <= q_pos)
    bias[...] = jnp.where(seen, 0.0, MASKED)
    reach[...] = jnp.where(begin < first, 1.0, 0.0)
    w_rows = WIN_DEV * rows
    w_pos = first - w_rows + lax.broadcasted_iota(jnp.int32, (w_rows, HD), 0)
    live[...] = jnp.where(w_pos >= begin[:1], 1.0, 0.0)
    for copy in large:
        copy.wait()

    def head_cols(h):
        return pl.ds(h * HD, HD)

    def scores(q, keys):
        return lax.dot_general(q, keys, (((1,), (1,)), ((), ())), preferred_element_type=jnp.float32)

    def spread(x, width):
        whole = [x] * (width // HD)
        if width % HD:
            whole.append(x[:, : width % HD])
        return jnp.concatenate(whole, axis=1)

    def mix(p, vals):
        return jnp.dot(p.astype(jnp.bfloat16), vals, preferred_element_type=jnp.float32)

    def stacked(t):
        heads = [t * GROUP + j for j in range(GROUP)]
        q = jnp.concatenate([q_ref[:, head_cols(h)] for h in heads], axis=0)
        fac = jnp.concatenate([lv[...] * scale_ref[h] for h in heads], axis=0)
        return q, fac

    def own_part(kv):
        keys = k_ref[:, head_cols(kv)]
        vals = v_ref[:, head_cols(kv)]
        vals = jnp.concatenate([vals, jnp.ones(vals.shape, vals.dtype)], axis=1)
        for i in range(PER // GROUP):
            t = kv * (PER // GROUP) + i
            q, fac = stacked(t)
            s = scores(q, keys).reshape(GROUP, rows, rows) + bias[...][None]
            s = s.reshape(GROUP * rows, rows)
            m = jnp.max(s, axis=1, keepdims=True)
            acc[t] = mix(jnp.exp2((s - m) * spread(fac, rows)), vals)
            top[t] = jnp.broadcast_to(m, top.shape[1:])

    def window_part(kv):
        alive = live[...]
        keys = kw[:, :, head_cols(kv)].reshape(w_rows, HD).astype(jnp.float32)
        keys = jnp.where(alive > 0, keys, k_ref[:16, head_cols(kv)].astype(jnp.float32)[:1])
        keys = keys.astype(jnp.bfloat16)
        vals = vw[:, :, head_cols(kv)].reshape(w_rows, HD).astype(jnp.float32)
        vals = jnp.concatenate([jnp.where(alive > 0, vals, 0.0), alive], axis=1).astype(jnp.bfloat16)
        reaching = jnp.concatenate([reach[...]] * GROUP, axis=0)
        reached = reaching > 0
        both_reached = spread(reaching, 2 * HD) > 0
        for i in range(PER // GROUP):
            t = kv * (PER // GROUP) + i
            q, fac = stacked(t)
            s = scores(q, keys)
            m_own = top[t]
            m_win = jnp.broadcast_to(jnp.max(s, axis=1, keepdims=True), m_own.shape)
            m = jnp.where(reached, jnp.maximum(m_own, m_win), m_own)
            mixed = mix(jnp.exp2((s - spread(m, w_rows)) * spread(fac, w_rows)), vals)
            kept = spread(jnp.exp2((m_own - m) * fac), 2 * HD)
            both = acc[t] * kept + jnp.where(both_reached, mixed, 0.0)
            out = (both[:, :HD] / both[:, HD:]).astype(o_ref.dtype)
            for j in range(GROUP):
                o_ref[:, head_cols(t * GROUP + j)] = out[j * rows : (j + 1) * rows]

    for step in range(HK):
        own_part(step)
        pass_on_far(step)
        if step:
            pass_on_near(step - 1)
    for step in range(HK):
        arrived(1, step)
        arrived(3, step)
        window_part(step)
        if step == 0:
            pass_on_near(HK - 1)

    for part in range(HK):

        @pl.when(to4)
        def _(part=part):
            sent(0, part)

        if relay:
            sent(1, part)
        else:

            @pl.when(to2)
            def _(part=part):
                sent(1, part)

        sent(2, part)
        sent(3, part)


def body(queries, keys, values, lengths, ssmax_scale):
    rows = queries.shape[0]
    n_ctx, n_grp = lax.axis_size("ctx"), lax.axis_size("grp")
    vmem = pl.BlockSpec(memory_space=pltpu.VMEM)
    hbm = pl.BlockSpec(memory_space=pltpu.HBM)
    window = pltpu.VMEM((WIN_DEV, rows, HK * HD), jnp.bfloat16)
    pairs = HQ * rows * (WIN_DEV + 1) * rows
    return pl.pallas_call(
        functools.partial(kernel, n_ctx, n_grp),
        out_shape=jax.ShapeDtypeStruct(queries.shape, queries.dtype),
        in_specs=[hbm] * 5,
        out_specs=vmem,
        scratch_shapes=[
            pltpu.SMEM(ssmax_scale.shape, ssmax_scale.dtype),
            pltpu.SMEM(lengths.shape, lengths.dtype),
            pltpu.VMEM(queries.shape, queries.dtype),
            pltpu.VMEM(keys.shape, keys.dtype),
            pltpu.VMEM(values.shape, values.dtype),
            window,
            window,
            pltpu.VMEM((rows, rows), jnp.float32),
            pltpu.VMEM((rows, HD), jnp.float32),
            pltpu.VMEM((WIN_DEV * rows, HD), jnp.float32),
            pltpu.VMEM((rows, HD), jnp.float32),
            pltpu.VMEM((HQ // GROUP, GROUP * rows, 2 * HD), jnp.float32),
            pltpu.VMEM((HQ // GROUP, GROUP * rows, HD), jnp.float32),
            pltpu.SemaphoreType.DMA((5,)),
            pltpu.SemaphoreType.DMA((4, HK, 2)),
            pltpu.SemaphoreType.DMA((4, HK, 2)),
        ],
        compiler_params=pltpu.CompilerParams(
            collective_id=0, has_side_effects=True, vmem_limit_bytes=48 * 1024 * 1024
        ),
        cost_estimate=pl.CostEstimate(
            flops=4 * pairs * HD, bytes_accessed=4 * queries.size, transcendentals=pairs
        ),
    )(*[pltpu.with_memory_space_constraint(x, pltpu.HBM) for x in (ssmax_scale, lengths, queries, keys, values)])


def solution(mesh):
    spec = P(("ctx", "grp"), None)
    return jax.shard_map(
        body,
        mesh=mesh,
        in_specs=(spec, spec, spec, P(), P()),
        out_specs=spec,
        check_vma=False,
    )
```

```python
import functools
import math

import jax
import jax.numpy as jnp
from jax import lax
from jax.experimental import pallas as pl
from jax.experimental.pallas import tpu as pltpu
from jax.sharding import PartitionSpec as P

HQ = 32
HK = 4
HD = 128
WIN_DEV = 4
PER = HQ // HK
GROUP = 4
MESH = pl.DeviceIdType.MESH
MASKED = -1e30


def kernel(
    n_ctx, n_grp, scale_hbm, len_hbm, q_hbm, k_hbm, v_hbm, o_ref,
    scale_ref, len_ref, q_ref, k_ref, v_ref,
    kw, vw, bias, reach, live, lv, acc, top, load_sem, send_sem, recv_sem,
):
    rows = q_ref.shape[0]
    loads = [
        pltpu.make_async_copy(src, dst, load_sem.at[i])
        for i, (src, dst) in enumerate(
            (
                (len_hbm, len_ref),
                (scale_hbm, scale_ref),
                (k_hbm, k_ref),
                (v_hbm, v_ref),
                (q_hbm, q_ref),
            )
        )
    ]
    for copy in loads:
        copy.start()
    small, large = loads[:2], loads[2:]
    n_dev = n_ctx * n_grp
    c = lax.axis_index("ctx")
    g = lax.axis_index("grp")
    me = c * n_grp + g
    core = lax.rem(g, 2)
    relay = n_grp == 4

    def at(lin):
        return (lin // n_grp, lin % n_grp)

    sibling = (c, g + 1 - 2 * core)
    across = (c, lax.rem(g + 2, 4))

    barrier = pltpu.get_barrier_semaphore()

    def greet(dev):
        pl.semaphore_signal(barrier, inc=1, device_id=dev, device_id_type=MESH)

    has4, to4 = me >= 4, me + 4 < n_dev
    has2, to2 = me >= 2, me + 2 < n_dev
    greet(sibling)
    count = 1 + has4.astype(jnp.int32) + to4.astype(jnp.int32)

    @pl.when(has4)
    def _():
        greet(at(me - 4))

    @pl.when(to4)
    def _():
        greet(at(me + 4))

    if relay:
        greet(across)
        count = count + 1
    else:
        count = count + has2.astype(jnp.int32) + to2.astype(jnp.int32)

        @pl.when(has2)
        def _():
            greet(at(me - 2))

        @pl.when(to2)
        def _():
            greet(at(me + 2))

    @pl.when(jnp.logical_not(has4))
    def _():
        kw[0] = jnp.zeros(kw.shape[1:], kw.dtype)
        vw[0] = jnp.zeros(vw.shape[1:], vw.dtype)

    if not relay:

        @pl.when(jnp.logical_not(has2))
        def _():
            kw[2] = jnp.zeros(kw.shape[1:], kw.dtype)
            vw[2] = jnp.zeros(vw.shape[1:], vw.dtype)

    pl.semaphore_wait(barrier, count)

    def copies(src_slot, dst_slot, kind, part, dev):
        cols = pl.ds(part * HD, HD)
        made = []
        for i, (own, win) in enumerate(((k_hbm, kw), (v_hbm, vw))):
            src = own.at[:, cols] if src_slot is None else win.at[src_slot, :, cols]
            made.append(
                pltpu.make_async_remote_copy(
                    src_ref=src,
                    dst_ref=win.at[dst_slot, :, cols],
                    send_sem=send_sem.at[kind, part, i],
                    recv_sem=recv_sem.at[dst_slot, part, i],
                    device_id=dev,
                    device_id_type=MESH,
                )
            )
        return made

    def start(*args):
        for copy in copies(*args):
            copy.start()

    def arrived(slot, part):
        for copy in copies(None, slot, 0, part, sibling):
            copy.wait_recv()

    def sent(kind, part):
        for copy in copies(None, 0, kind, part, sibling):
            copy.wait_send()

    first_chip = g < 2
    def launch(part):
        @pl.when(to4)
        def _():
            start(None, 0, 0, part, at(me + 4))

        if relay:

            @pl.when(first_chip)
            def _():
                start(None, 2, 1, part, across)

        else:

            @pl.when(to2)
            def _():
                start(None, 2, 1, part, at(me + 2))

    def settle(part):
        @pl.when(to4)
        def _():
            sent(0, part)

        @pl.when(first_chip if relay else to2)
        def _():
            sent(1, part)

    for part in range(2):
        launch(part)

    @pl.when(core == 0)
    def _():
        for part in range(HK):
            start(None, 3, 2, part, sibling)

    def pass_on_far(part):
        @pl.when(has4)
        def _():
            arrived(0, part)

        if relay:

            @pl.when(jnp.logical_not(first_chip))
            def _():
                start(0, 2, 1, part, across)

        @pl.when(core == 1)
        def _():
            start(0, 1, 2, part, sibling)

    def pass_on_near(part):
        if relay:
            arrived(2, part)
        else:

            @pl.when(has2)
            def _():
                arrived(2, part)

        @pl.when(core == 0)
        def _():
            start(2, 1, 3, part, sibling)

        @pl.when(core == 1)
        def _():
            start(2, 3, 3, part, sibling)

    for copy in small:
        copy.wait()
    first = me * rows
    pos = first + lax.broadcasted_iota(jnp.int32, (rows, HD), 0)

    def doc(j, carry):
        total, begin = carry
        total = total + len_ref[j]
        return total, jnp.where(total <= pos, total, begin)

    _, begin = lax.fori_loop(0, len_ref.shape[0], doc, (jnp.int32(0), jnp.zeros_like(pos)))
    visible = pos - begin + 1
    factor = jnp.log(visible.astype(jnp.float32)) * (math.log2(math.e) / math.sqrt(HD))
    lv[...] = jnp.where(visible == 1, 1.0, factor)
    k_pos = first + lax.broadcasted_iota(jnp.int32, (rows, rows), 1)
    q_pos = first + lax.broadcasted_iota(jnp.int32, (rows, rows), 0)
    seen = (k_pos >= jnp.broadcast_to(begin[:, :1], (rows, rows))) & (k_pos <= q_pos)
    bias[...] = jnp.where(seen, 0.0, MASKED)
    reach[...] = jnp.where(begin < first, 1.0, 0.0)
    w_rows = WIN_DEV * rows
    w_pos = first - w_rows + lax.broadcasted_iota(jnp.int32, (w_rows, HD), 0)
    live[...] = jnp.where(w_pos >= begin[:1], 1.0, 0.0)
    for copy in large:
        copy.wait()

    def head_cols(h):
        return pl.ds(h * HD, HD)

    def scores(q, keys):
        return lax.dot_general(q, keys, (((1,), (1,)), ((), ())), preferred_element_type=jnp.float32)

    def spread(x, width):
        whole = [x] * (width // HD)
        if width % HD:
            whole.append(x[:, : width % HD])
        return jnp.concatenate(whole, axis=1)

    def mix(p, vals):
        return jnp.dot(p.astype(jnp.bfloat16), vals, preferred_element_type=jnp.float32)

    def stacked(t):
        heads = [t * GROUP + j for j in range(GROUP)]
        q = jnp.concatenate([q_ref[:, head_cols(h)] for h in heads], axis=0)
        fac = jnp.concatenate([lv[...] * scale_ref[h] for h in heads], axis=0)
        return q, fac

    def own_part(kv, tiles=range(PER // GROUP)):
        keys = k_ref[:, head_cols(kv)]
        vals = v_ref[:, head_cols(kv)]
        vals = jnp.concatenate([vals, jnp.ones(vals.shape, vals.dtype)], axis=1)
        for i in tiles:
            t = kv * (PER // GROUP) + i
            q, fac = stacked(t)
            s = scores(q, keys).reshape(GROUP, rows, rows) + bias[...][None]
            s = s.reshape(GROUP * rows, rows)
            m = jnp.max(s, axis=1, keepdims=True)
            acc[t] = mix(jnp.exp2((s - m) * spread(fac, rows)), vals)
            top[t] = jnp.broadcast_to(m, top.shape[1:])

    def window_part(kv):
        alive = live[...]
        keys = kw[:, :, head_cols(kv)].reshape(w_rows, HD).astype(jnp.float32)
        keys = jnp.where(alive > 0, keys, k_ref[:16, head_cols(kv)].astype(jnp.float32)[:1])
        keys = keys.astype(jnp.bfloat16)
        vals = vw[:, :, head_cols(kv)].reshape(w_rows, HD).astype(jnp.float32)
        vals = jnp.concatenate([jnp.where(alive > 0, vals, 0.0), alive], axis=1).astype(jnp.bfloat16)
        reaching = jnp.concatenate([reach[...]] * GROUP, axis=0)
        reached = reaching > 0
        both_reached = spread(reaching, 2 * HD) > 0
        for i in range(PER // GROUP):
            t = kv * (PER // GROUP) + i
            q, fac = stacked(t)
            s = scores(q, keys)
            m_own = top[t]
            m_win = jnp.broadcast_to(jnp.max(s, axis=1, keepdims=True), m_own.shape)
            m = jnp.where(reached, jnp.maximum(m_own, m_win), m_own)
            mixed = mix(jnp.exp2((s - spread(m, w_rows)) * spread(fac, w_rows)), vals)
            kept = spread(jnp.exp2((m_own - m) * fac), 2 * HD)
            both = acc[t] * kept + jnp.where(both_reached, mixed, 0.0)
            out = (both[:, :HD] / both[:, HD:]).astype(o_ref.dtype)
            for j in range(GROUP):
                o_ref[:, head_cols(t * GROUP + j)] = out[j * rows : (j + 1) * rows]

    own_part(0)
    settle(0)
    launch(2)
    pass_on_far(0)
    own_part(1)
    settle(1)
    launch(3)
    own_part(2, (0,))
    pass_on_far(1)
    own_part(2, (1,))
    pass_on_near(0)
    own_part(3, (0,))
    pass_on_far(2)
    own_part(3, (1,))
    pass_on_near(1)
    for step in range(HK):
        arrived(1, step)
        arrived(3, step)
        window_part(step)
        if step == 0:
            pass_on_near(2)
            pass_on_far(3)
        if step == 1:
            pass_on_near(3)

    settle(2)
    settle(3)
    if relay:

        @pl.when(jnp.logical_not(first_chip))
        def _():
            for part in range(HK):
                sent(1, part)

    for part in range(HK):
        sent(2, part)
        sent(3, part)


def body(queries, keys, values, lengths, ssmax_scale):
    rows = queries.shape[0]
    n_ctx, n_grp = lax.axis_size("ctx"), lax.axis_size("grp")
    vmem = pl.BlockSpec(memory_space=pltpu.VMEM)
    hbm = pl.BlockSpec(memory_space=pltpu.HBM)
    window = pltpu.VMEM((WIN_DEV, rows, HK * HD), jnp.bfloat16)
    pairs = HQ * rows * (WIN_DEV + 1) * rows
    return pl.pallas_call(
        functools.partial(kernel, n_ctx, n_grp),
        out_shape=jax.ShapeDtypeStruct(queries.shape, queries.dtype),
        in_specs=[hbm] * 5,
        out_specs=vmem,
        scratch_shapes=[
            pltpu.SMEM(ssmax_scale.shape, ssmax_scale.dtype),
            pltpu.SMEM(lengths.shape, lengths.dtype),
            pltpu.VMEM(queries.shape, queries.dtype),
            pltpu.VMEM(keys.shape, keys.dtype),
            pltpu.VMEM(values.shape, values.dtype),
            window,
            window,
            pltpu.VMEM((rows, rows), jnp.float32),
            pltpu.VMEM((rows, HD), jnp.float32),
            pltpu.VMEM((WIN_DEV * rows, HD), jnp.float32),
            pltpu.VMEM((rows, HD), jnp.float32),
            pltpu.VMEM((HQ // GROUP, GROUP * rows, 2 * HD), jnp.float32),
            pltpu.VMEM((HQ // GROUP, GROUP * rows, HD), jnp.float32),
            pltpu.SemaphoreType.DMA((5,)),
            pltpu.SemaphoreType.DMA((4, HK, 2)),
            pltpu.SemaphoreType.DMA((4, HK, 2)),
        ],
        compiler_params=pltpu.CompilerParams(
            collective_id=0, has_side_effects=True, vmem_limit_bytes=48 * 1024 * 1024
        ),
        cost_estimate=pl.CostEstimate(
            flops=4 * pairs * HD, bytes_accessed=4 * queries.size, transcendentals=pairs
        ),
    )(*[pltpu.with_memory_space_constraint(x, pltpu.HBM) for x in (ssmax_scale, lengths, queries, keys, values)])


def solution(mesh):
    spec = P(("ctx", "grp"), None)
    return jax.shard_map(
        body,
        mesh=mesh,
        in_specs=(spec, spec, spec, P(), P()),
        out_specs=spec,
        check_vma=False,
    )
```

```python
import functools
import math

import jax
import jax.numpy as jnp
from jax import lax
from jax.experimental import pallas as pl
from jax.experimental.pallas import tpu as pltpu
from jax.sharding import PartitionSpec as P

HQ = 32
HK = 4
HD = 128
WIN_DEV = 4
PER = HQ // HK
GROUP = 4
MESH = pl.DeviceIdType.MESH
MASKED = -1e30


def kernel(
    n_ctx, n_grp, scale_hbm, len_hbm, q_hbm, k_hbm, v_hbm, o_ref,
    scale_ref, len_ref, q_ref, k_ref, v_ref,
    kw, vw, bias, reach, live, lv, acc, top, load_sem, send_sem, recv_sem,
):
    rows = q_ref.shape[0]
    loads = [
        pltpu.make_async_copy(src, dst, load_sem.at[i])
        for i, (src, dst) in enumerate(
            (
                (len_hbm, len_ref),
                (scale_hbm, scale_ref),
                (k_hbm, k_ref),
                (v_hbm, v_ref),
                (q_hbm, q_ref),
            )
        )
    ]
    for copy in loads:
        copy.start()
    small, large = loads[:2], loads[2:]
    n_dev = n_ctx * n_grp
    c = lax.axis_index("ctx")
    g = lax.axis_index("grp")
    me = c * n_grp + g
    core = lax.rem(g, 2)
    relay = n_grp == 4

    def at(lin):
        return (lin // n_grp, lin % n_grp)

    sibling = (c, g + 1 - 2 * core)
    across = (c, lax.rem(g + 2, 4))

    barrier = pltpu.get_barrier_semaphore()

    def greet(dev):
        pl.semaphore_signal(barrier, inc=1, device_id=dev, device_id_type=MESH)

    has4, to4 = me >= 4, me + 4 < n_dev
    has2, to2 = me >= 2, me + 2 < n_dev
    greet(sibling)
    count = 1 + has4.astype(jnp.int32) + to4.astype(jnp.int32)

    @pl.when(has4)
    def _():
        greet(at(me - 4))

    @pl.when(to4)
    def _():
        greet(at(me + 4))

    if relay:
        greet(across)
        count = count + 1
    else:
        count = count + has2.astype(jnp.int32) + to2.astype(jnp.int32)

        @pl.when(has2)
        def _():
            greet(at(me - 2))

        @pl.when(to2)
        def _():
            greet(at(me + 2))

    @pl.when(jnp.logical_not(has4))
    def _():
        kw[0] = jnp.zeros(kw.shape[1:], kw.dtype)
        vw[0] = jnp.zeros(vw.shape[1:], vw.dtype)

    if not relay:

        @pl.when(jnp.logical_not(has2))
        def _():
            kw[2] = jnp.zeros(kw.shape[1:], kw.dtype)
            vw[2] = jnp.zeros(vw.shape[1:], vw.dtype)

    pl.semaphore_wait(barrier, count)

    def copies(src_slot, dst_slot, kind, part, dev):
        cols = pl.ds(part * HD, HD)
        made = []
        for i, (own, win) in enumerate(((k_hbm, kw), (v_hbm, vw))):
            src = own.at[:, cols] if src_slot is None else win.at[src_slot, :, cols]
            made.append(
                pltpu.make_async_remote_copy(
                    src_ref=src,
                    dst_ref=win.at[dst_slot, :, cols],
                    send_sem=send_sem.at[kind, part, i],
                    recv_sem=recv_sem.at[dst_slot, part, i],
                    device_id=dev,
                    device_id_type=MESH,
                )
            )
        return made

    def start(*args):
        for copy in copies(*args):
            copy.start()

    def arrived(slot, part):
        for copy in copies(None, slot, 0, part, sibling):
            copy.wait_recv()

    def sent(kind, part):
        for copy in copies(None, 0, kind, part, sibling):
            copy.wait_send()

    first_chip = g < 2
    def launch(part):
        @pl.when(to4)
        def _():
            start(None, 0, 0, part, at(me + 4))

        if relay:

            @pl.when(first_chip)
            def _():
                start(None, 2, 1, part, across)

        else:

            @pl.when(to2)
            def _():
                start(None, 2, 1, part, at(me + 2))

    def settle(part):
        @pl.when(to4)
        def _():
            sent(0, part)

        @pl.when(first_chip if relay else to2)
        def _():
            sent(1, part)

    for part in range(2):
        launch(part)

    @pl.when(core == 0)
    def _():
        for part in range(HK):
            start(None, 3, 2, part, sibling)

    def pass_on_far(part):
        @pl.when(has4)
        def _():
            arrived(0, part)

        if relay:

            @pl.when(jnp.logical_not(first_chip))
            def _():
                start(0, 2, 1, part, across)

        @pl.when(core == 1)
        def _():
            start(0, 1, 2, part, sibling)

    def pass_on_near(part):
        if relay:
            arrived(2, part)
        else:

            @pl.when(has2)
            def _():
                arrived(2, part)

        @pl.when(core == 0)
        def _():
            start(2, 1, 3, part, sibling)

        @pl.when(core == 1)
        def _():
            start(2, 3, 3, part, sibling)

    for copy in small:
        copy.wait()
    first = me * rows
    pos = first + lax.broadcasted_iota(jnp.int32, (rows, HD), 0)

    def doc(j, carry):
        total, begin = carry
        total = total + len_ref[j]
        return total, jnp.where(total <= pos, total, begin)

    _, begin = lax.fori_loop(0, len_ref.shape[0], doc, (jnp.int32(0), jnp.zeros_like(pos)))
    visible = pos - begin + 1
    factor = jnp.log(visible.astype(jnp.float32)) * (math.log2(math.e) / math.sqrt(HD))
    lv[...] = jnp.where(visible == 1, 1.0, factor)
    k_pos = first + lax.broadcasted_iota(jnp.int32, (rows, rows), 1)
    q_pos = first + lax.broadcasted_iota(jnp.int32, (rows, rows), 0)
    seen = (k_pos >= jnp.broadcast_to(begin[:, :1], (rows, rows))) & (k_pos <= q_pos)
    bias[...] = jnp.where(seen, 0.0, MASKED)
    reach[...] = jnp.where(begin < first, 1.0, 0.0)
    w_rows = WIN_DEV * rows
    w_pos = first - w_rows + lax.broadcasted_iota(jnp.int32, (w_rows, HD), 0)
    live[...] = jnp.where(w_pos >= begin[:1], 1.0, 0.0)
    for copy in large:
        copy.wait()

    def head_cols(h):
        return pl.ds(h * HD, HD)

    def scores(q, keys):
        return lax.dot_general(q, keys, (((1,), (1,)), ((), ())), preferred_element_type=jnp.float32)

    def spread(x, width):
        whole = [x] * (width // HD)
        if width % HD:
            whole.append(x[:, : width % HD])
        return jnp.concatenate(whole, axis=1)

    def mix(p, vals):
        return jnp.dot(p.astype(jnp.bfloat16), vals, preferred_element_type=jnp.float32)

    def stacked(t):
        heads = [t * GROUP + j for j in range(GROUP)]
        q = jnp.concatenate([q_ref[:, head_cols(h)] for h in heads], axis=0)
        fac = jnp.concatenate([lv[...] * scale_ref[h] for h in heads], axis=0)
        return q, fac

    def own_part(kv, tiles=range(PER // GROUP)):
        keys = k_ref[:, head_cols(kv)]
        vals = v_ref[:, head_cols(kv)]
        vals = jnp.concatenate([vals, jnp.ones(vals.shape, vals.dtype)], axis=1)
        for i in tiles:
            t = kv * (PER // GROUP) + i
            q, fac = stacked(t)
            s = scores(q, keys).reshape(GROUP, rows, rows) + bias[...][None]
            s = s.reshape(GROUP * rows, rows)
            m = jnp.max(s, axis=1, keepdims=True)
            acc[t] = mix(jnp.exp2((s - m) * spread(fac, rows)), vals)
            top[t] = jnp.broadcast_to(m, top.shape[1:])

    def window_part(kv, tiles=range(PER // GROUP)):
        alive = live[...]
        keys = kw[:, :, head_cols(kv)].reshape(w_rows, HD).astype(jnp.float32)
        keys = jnp.where(alive > 0, keys, k_ref[:16, head_cols(kv)].astype(jnp.float32)[:1])
        keys = keys.astype(jnp.bfloat16)
        vals = vw[:, :, head_cols(kv)].reshape(w_rows, HD).astype(jnp.float32)
        vals = jnp.concatenate([jnp.where(alive > 0, vals, 0.0), alive], axis=1).astype(jnp.bfloat16)
        reaching = jnp.concatenate([reach[...]] * GROUP, axis=0)
        reached = reaching > 0
        both_reached = spread(reaching, 2 * HD) > 0
        for i in tiles:
            t = kv * (PER // GROUP) + i
            q, fac = stacked(t)
            s = scores(q, keys)
            m_own = top[t]
            m_win = jnp.broadcast_to(jnp.max(s, axis=1, keepdims=True), m_own.shape)
            m = jnp.where(reached, jnp.maximum(m_own, m_win), m_own)
            mixed = mix(jnp.exp2((s - spread(m, w_rows)) * spread(fac, w_rows)), vals)
            kept = spread(jnp.exp2((m_own - m) * fac), 2 * HD)
            both = acc[t] * kept + jnp.where(both_reached, mixed, 0.0)
            out = (both[:, :HD] / both[:, HD:]).astype(o_ref.dtype)
            for j in range(GROUP):
                o_ref[:, head_cols(t * GROUP + j)] = out[j * rows : (j + 1) * rows]

    def ready(part):
        arrived(1, part)
        arrived(3, part)

    own_part(0)
    settle(0)
    launch(2)
    pass_on_far(0)
    own_part(1, (0,))
    settle(1)
    launch(3)
    own_part(1, (1,))
    pass_on_far(1)
    own_part(2)
    pass_on_near(0)
    pass_on_far(2)
    own_part(3)
    ready(0)
    window_part(0, (0,))
    pass_on_far(3)
    pass_on_near(1)
    window_part(0, (1,))
    pass_on_near(2)
    ready(1)
    window_part(1, (0,))
    pass_on_near(3)
    window_part(1, (1,))
    for step in range(2, HK):
        ready(step)
        window_part(step)

    settle(2)
    settle(3)
    if relay:

        @pl.when(jnp.logical_not(first_chip))
        def _():
            for part in range(HK):
                sent(1, part)

    for part in range(HK):
        sent(2, part)
        sent(3, part)


def body(queries, keys, values, lengths, ssmax_scale):
    rows = queries.shape[0]
    n_ctx, n_grp = lax.axis_size("ctx"), lax.axis_size("grp")
    vmem = pl.BlockSpec(memory_space=pltpu.VMEM)
    hbm = pl.BlockSpec(memory_space=pltpu.HBM)
    window = pltpu.VMEM((WIN_DEV, rows, HK * HD), jnp.bfloat16)
    pairs = HQ * rows * (WIN_DEV + 1) * rows
    return pl.pallas_call(
        functools.partial(kernel, n_ctx, n_grp),
        out_shape=jax.ShapeDtypeStruct(queries.shape, queries.dtype),
        in_specs=[hbm] * 5,
        out_specs=vmem,
        scratch_shapes=[
            pltpu.SMEM(ssmax_scale.shape, ssmax_scale.dtype),
            pltpu.SMEM(lengths.shape, lengths.dtype),
            pltpu.VMEM(queries.shape, queries.dtype),
            pltpu.VMEM(keys.shape, keys.dtype),
            pltpu.VMEM(values.shape, values.dtype),
            window,
            window,
            pltpu.VMEM((rows, rows), jnp.float32),
            pltpu.VMEM((rows, HD), jnp.float32),
            pltpu.VMEM((WIN_DEV * rows, HD), jnp.float32),
            pltpu.VMEM((rows, HD), jnp.float32),
            pltpu.VMEM((HQ // GROUP, GROUP * rows, 2 * HD), jnp.float32),
            pltpu.VMEM((HQ // GROUP, GROUP * rows, HD), jnp.float32),
            pltpu.SemaphoreType.DMA((5,)),
            pltpu.SemaphoreType.DMA((4, HK, 2)),
            pltpu.SemaphoreType.DMA((4, HK, 2)),
        ],
        compiler_params=pltpu.CompilerParams(
            collective_id=0, has_side_effects=True, vmem_limit_bytes=48 * 1024 * 1024
        ),
        cost_estimate=pl.CostEstimate(
            flops=4 * pairs * HD, bytes_accessed=4 * queries.size, transcendentals=pairs
        ),
    )(*[pltpu.with_memory_space_constraint(x, pltpu.HBM) for x in (ssmax_scale, lengths, queries, keys, values)])


def solution(mesh):
    spec = P(("ctx", "grp"), None)
    return jax.shard_map(
        body,
        mesh=mesh,
        in_specs=(spec, spec, spec, P(), P()),
        out_specs=spec,
        check_vma=False,
    )
```

```python
import functools
import math

import jax
import jax.numpy as jnp
from jax import lax
from jax.experimental import pallas as pl
from jax.experimental.pallas import tpu as pltpu
from jax.sharding import PartitionSpec as P

HQ = 32
HK = 4
HD = 128
WIN_DEV = 4
PER = HQ // HK
GROUP = 4
MESH = pl.DeviceIdType.MESH
MASKED = -1e30


def kernel(
    n_ctx, n_grp, scale_hbm, len_hbm, q_hbm, k_hbm, v_hbm, o_ref,
    scale_ref, len_ref, q_ref, k_ref, v_ref,
    kw, vw, bias, reach, live, lv, acc, top, load_sem, send_sem, recv_sem,
):
    rows = q_ref.shape[0]
    loads = [
        pltpu.make_async_copy(src, dst, load_sem.at[i])
        for i, (src, dst) in enumerate(
            (
                (len_hbm, len_ref),
                (scale_hbm, scale_ref),
                (k_hbm, k_ref),
                (v_hbm, v_ref),
                (q_hbm, q_ref),
            )
        )
    ]
    for copy in loads:
        copy.start()
    small, large = loads[:2], loads[2:]
    n_dev = n_ctx * n_grp
    c = lax.axis_index("ctx")
    g = lax.axis_index("grp")
    me = c * n_grp + g
    core = lax.rem(g, 2)
    relay = n_grp == 4

    def at(lin):
        return (lin // n_grp, lin % n_grp)

    sibling = (c, g + 1 - 2 * core)
    across = (c, lax.rem(g + 2, 4))

    barrier = pltpu.get_barrier_semaphore()

    def greet(dev):
        pl.semaphore_signal(barrier, inc=1, device_id=dev, device_id_type=MESH)

    has4, to4 = me >= 4, me + 4 < n_dev
    has2, to2 = me >= 2, me + 2 < n_dev
    greet(sibling)
    count = 1 + has4.astype(jnp.int32) + to4.astype(jnp.int32)

    @pl.when(has4)
    def _():
        greet(at(me - 4))

    @pl.when(to4)
    def _():
        greet(at(me + 4))

    if relay:
        greet(across)
        count = count + 1
    else:
        count = count + has2.astype(jnp.int32) + to2.astype(jnp.int32)

        @pl.when(has2)
        def _():
            greet(at(me - 2))

        @pl.when(to2)
        def _():
            greet(at(me + 2))

    @pl.when(jnp.logical_not(has4))
    def _():
        kw[0] = jnp.zeros(kw.shape[1:], kw.dtype)
        vw[0] = jnp.zeros(vw.shape[1:], vw.dtype)

    if not relay:

        @pl.when(jnp.logical_not(has2))
        def _():
            kw[2] = jnp.zeros(kw.shape[1:], kw.dtype)
            vw[2] = jnp.zeros(vw.shape[1:], vw.dtype)

    pl.semaphore_wait(barrier, count)

    def copies(src_slot, dst_slot, kind, part, dev):
        cols = pl.ds(part * HD, HD)
        made = []
        for i, (own, win) in enumerate(((k_hbm, kw), (v_hbm, vw))):
            src = own.at[:, cols] if src_slot is None else win.at[src_slot, :, cols]
            made.append(
                pltpu.make_async_remote_copy(
                    src_ref=src,
                    dst_ref=win.at[dst_slot, :, cols],
                    send_sem=send_sem.at[kind, part, i],
                    recv_sem=recv_sem.at[dst_slot, part, i],
                    device_id=dev,
                    device_id_type=MESH,
                )
            )
        return made

    def start(*args):
        for copy in copies(*args):
            copy.start()

    def arrived(slot, part):
        for copy in copies(None, slot, 0, part, sibling):
            copy.wait_recv()

    def sent(kind, part):
        for copy in copies(None, 0, kind, part, sibling):
            copy.wait_send()

    first_chip = g < 2
    def launch(part):
        @pl.when(to4)
        def _():
            start(None, 0, 0, part, at(me + 4))

        if relay:

            @pl.when(first_chip)
            def _():
                start(None, 2, 1, part, across)

        else:

            @pl.when(to2)
            def _():
                start(None, 2, 1, part, at(me + 2))

    def settle(part):
        @pl.when(to4)
        def _():
            sent(0, part)

        @pl.when(first_chip if relay else to2)
        def _():
            sent(1, part)

    for part in range(2):
        launch(part)

    @pl.when(core == 0)
    def _():
        for part in range(HK):
            start(None, 3, 2, part, sibling)

    def pass_on_far(part):
        @pl.when(has4)
        def _():
            arrived(0, part)

        if relay:

            @pl.when(jnp.logical_not(first_chip))
            def _():
                start(0, 2, 1, part, across)

        @pl.when(core == 1)
        def _():
            start(0, 1, 2, part, sibling)

    def pass_on_near(part):
        if relay:
            arrived(2, part)
        else:

            @pl.when(has2)
            def _():
                arrived(2, part)

        @pl.when(core == 0)
        def _():
            start(2, 1, 3, part, sibling)

        @pl.when(core == 1)
        def _():
            start(2, 3, 3, part, sibling)

    for copy in small:
        copy.wait()
    first = me * rows
    pos = first + lax.broadcasted_iota(jnp.int32, (rows, HD), 0)

    def doc(j, carry):
        total, begin = carry
        total = total + len_ref[j]
        return total, jnp.where(total <= pos, total, begin)

    _, begin = lax.fori_loop(0, len_ref.shape[0], doc, (jnp.int32(0), jnp.zeros_like(pos)))
    visible = pos - begin + 1
    factor = jnp.log(visible.astype(jnp.float32)) * (math.log2(math.e) / math.sqrt(HD))
    lv[...] = jnp.where(visible == 1, 1.0, factor)
    k_pos = first + lax.broadcasted_iota(jnp.int32, (rows, rows), 1)
    q_pos = first + lax.broadcasted_iota(jnp.int32, (rows, rows), 0)
    seen = (k_pos >= jnp.broadcast_to(begin[:, :1], (rows, rows))) & (k_pos <= q_pos)
    bias[...] = jnp.where(seen, 0.0, MASKED)
    reach[...] = jnp.where(begin < first, 1.0, 0.0)
    w_rows = WIN_DEV * rows
    w_pos = first - w_rows + lax.broadcasted_iota(jnp.int32, (w_rows, HD), 0)
    live[...] = jnp.where(w_pos >= begin[:1], 1.0, 0.0).astype(live.dtype)
    for copy in large:
        copy.wait()

    def head_cols(h):
        return pl.ds(h * HD, HD)

    def scores(q, keys):
        return lax.dot_general(q, keys, (((1,), (1,)), ((), ())), preferred_element_type=jnp.float32)

    def spread(x, width):
        whole = [x] * (width // HD)
        if width % HD:
            whole.append(x[:, : width % HD])
        return jnp.concatenate(whole, axis=1)

    def mix(p, vals):
        return jnp.dot(p.astype(jnp.bfloat16), vals, preferred_element_type=jnp.float32)

    def stacked(t):
        heads = [t * GROUP + j for j in range(GROUP)]
        q = jnp.concatenate([q_ref[:, head_cols(h)] for h in heads], axis=0)
        fac = jnp.concatenate([lv[...] * scale_ref[h] for h in heads], axis=0)
        return q, fac

    def own_part(kv, tiles=range(PER // GROUP)):
        keys = k_ref[:, head_cols(kv)]
        vals = v_ref[:, head_cols(kv)]
        vals = jnp.concatenate([vals, jnp.ones(vals.shape, vals.dtype)], axis=1)
        for i in tiles:
            t = kv * (PER // GROUP) + i
            q, fac = stacked(t)
            s = scores(q, keys).reshape(GROUP, rows, rows) + bias[...][None]
            s = s.reshape(GROUP * rows, rows)
            m = jnp.max(s, axis=1, keepdims=True)
            acc[t] = mix(jnp.exp2((s - m) * spread(fac, rows)), vals)
            top[t] = jnp.broadcast_to(m, top.shape[1:])

    def window_part(kv):
        alive = live[...]
        stand_in = k_ref[:16, head_cols(kv)][:1] * (1 - alive)
        keys = kw[:, :, head_cols(kv)].reshape(w_rows, HD) * alive + stand_in
        vals = vw[:, :, head_cols(kv)].reshape(w_rows, HD) * alive
        vals = jnp.concatenate([vals, alive], axis=1)
        reaching = jnp.concatenate([reach[...]] * GROUP, axis=0)
        reached = reaching > 0
        both_reached = spread(reaching, 2 * HD) > 0
        for i in range(PER // GROUP):
            t = kv * (PER // GROUP) + i
            q, fac = stacked(t)
            s = scores(q, keys)
            m_own = top[t]
            m_win = jnp.broadcast_to(jnp.max(s, axis=1, keepdims=True), m_own.shape)
            m = jnp.where(reached, jnp.maximum(m_own, m_win), m_own)
            mixed = mix(jnp.exp2((s - spread(m, w_rows)) * spread(fac, w_rows)), vals)
            kept = spread(jnp.exp2((m_own - m) * fac), 2 * HD)
            both = acc[t] * kept + jnp.where(both_reached, mixed, 0.0)
            out = (both[:, :HD] / both[:, HD:]).astype(o_ref.dtype)
            for j in range(GROUP):
                o_ref[:, head_cols(t * GROUP + j)] = out[j * rows : (j + 1) * rows]

    own_part(0)
    settle(0)
    launch(2)
    pass_on_far(0)
    own_part(1)
    settle(1)
    launch(3)
    own_part(2, (0,))
    pass_on_far(1)
    own_part(2, (1,))
    pass_on_near(0)
    own_part(3, (0,))
    pass_on_far(2)
    own_part(3, (1,))
    pass_on_near(1)
    for step in range(HK):
        arrived(1, step)
        arrived(3, step)
        window_part(step)
        if step == 0:
            pass_on_near(2)
            pass_on_far(3)
        if step == 1:
            pass_on_near(3)

    settle(2)
    settle(3)
    if relay:

        @pl.when(jnp.logical_not(first_chip))
        def _():
            for part in range(HK):
                sent(1, part)

    for part in range(HK):
        sent(2, part)
        sent(3, part)


def body(queries, keys, values, lengths, ssmax_scale):
    rows = queries.shape[0]
    n_ctx, n_grp = lax.axis_size("ctx"), lax.axis_size("grp")
    vmem = pl.BlockSpec(memory_space=pltpu.VMEM)
    hbm = pl.BlockSpec(memory_space=pltpu.HBM)
    window = pltpu.VMEM((WIN_DEV, rows, HK * HD), jnp.bfloat16)
    pairs = HQ * rows * (WIN_DEV + 1) * rows
    return pl.pallas_call(
        functools.partial(kernel, n_ctx, n_grp),
        out_shape=jax.ShapeDtypeStruct(queries.shape, queries.dtype),
        in_specs=[hbm] * 5,
        out_specs=vmem,
        scratch_shapes=[
            pltpu.SMEM(ssmax_scale.shape, ssmax_scale.dtype),
            pltpu.SMEM(lengths.shape, lengths.dtype),
            pltpu.VMEM(queries.shape, queries.dtype),
            pltpu.VMEM(keys.shape, keys.dtype),
            pltpu.VMEM(values.shape, values.dtype),
            window,
            window,
            pltpu.VMEM((rows, rows), jnp.float32),
            pltpu.VMEM((rows, HD), jnp.float32),
            pltpu.VMEM((WIN_DEV * rows, HD), jnp.bfloat16),
            pltpu.VMEM((rows, HD), jnp.float32),
            pltpu.VMEM((HQ // GROUP, GROUP * rows, 2 * HD), jnp.float32),
            pltpu.VMEM((HQ // GROUP, GROUP * rows, HD), jnp.float32),
            pltpu.SemaphoreType.DMA((5,)),
            pltpu.SemaphoreType.DMA((4, HK, 2)),
            pltpu.SemaphoreType.DMA((4, HK, 2)),
        ],
        compiler_params=pltpu.CompilerParams(
            collective_id=0, has_side_effects=True, vmem_limit_bytes=48 * 1024 * 1024
        ),
        cost_estimate=pl.CostEstimate(
            flops=4 * pairs * HD, bytes_accessed=4 * queries.size, transcendentals=pairs
        ),
    )(*[pltpu.with_memory_space_constraint(x, pltpu.HBM) for x in (ssmax_scale, lengths, queries, keys, values)])


def solution(mesh):
    spec = P(("ctx", "grp"), None)
    return jax.shard_map(
        body,
        mesh=mesh,
        in_specs=(spec, spec, spec, P(), P()),
        out_specs=spec,
        check_vma=False,
    )
```

```python
import functools
import math

import jax
import jax.numpy as jnp
from jax import lax
from jax.experimental import pallas as pl
from jax.experimental.pallas import tpu as pltpu
from jax.sharding import PartitionSpec as P

HQ = 32
HK = 4
HD = 128
WIN_DEV = 4
PER = HQ // HK
GROUP = 8
MESH = pl.DeviceIdType.MESH
MASKED = -1e30


def kernel(
    n_ctx, n_grp, scale_hbm, len_hbm, q_hbm, k_hbm, v_hbm, o_ref,
    scale_ref, len_ref, q_ref, k_ref, v_ref,
    kw, vw, bias, reach, live, lv, acc, top, load_sem, send_sem, recv_sem,
):
    rows = q_ref.shape[0]
    loads = [
        pltpu.make_async_copy(src, dst, load_sem.at[i])
        for i, (src, dst) in enumerate(
            (
                (len_hbm, len_ref),
                (scale_hbm, scale_ref),
                (k_hbm, k_ref),
                (v_hbm, v_ref),
                (q_hbm, q_ref),
            )
        )
    ]
    for copy in loads:
        copy.start()
    small, large = loads[:2], loads[2:]
    n_dev = n_ctx * n_grp
    c = lax.axis_index("ctx")
    g = lax.axis_index("grp")
    me = c * n_grp + g
    core = lax.rem(g, 2)
    relay = n_grp == 4

    def at(lin):
        return (lin // n_grp, lin % n_grp)

    sibling = (c, g + 1 - 2 * core)
    across = (c, lax.rem(g + 2, 4))

    barrier = pltpu.get_barrier_semaphore()

    def greet(dev):
        pl.semaphore_signal(barrier, inc=1, device_id=dev, device_id_type=MESH)

    has4, to4 = me >= 4, me + 4 < n_dev
    has2, to2 = me >= 2, me + 2 < n_dev
    greet(sibling)
    count = 1 + has4.astype(jnp.int32) + to4.astype(jnp.int32)

    @pl.when(has4)
    def _():
        greet(at(me - 4))

    @pl.when(to4)
    def _():
        greet(at(me + 4))

    if relay:
        greet(across)
        count = count + 1
    else:
        count = count + has2.astype(jnp.int32) + to2.astype(jnp.int32)

        @pl.when(has2)
        def _():
            greet(at(me - 2))

        @pl.when(to2)
        def _():
            greet(at(me + 2))

    @pl.when(jnp.logical_not(has4))
    def _():
        kw[0] = jnp.zeros(kw.shape[1:], kw.dtype)
        vw[0] = jnp.zeros(vw.shape[1:], vw.dtype)

    if not relay:

        @pl.when(jnp.logical_not(has2))
        def _():
            kw[2] = jnp.zeros(kw.shape[1:], kw.dtype)
            vw[2] = jnp.zeros(vw.shape[1:], vw.dtype)

    pl.semaphore_wait(barrier, count)

    def copies(src_slot, dst_slot, kind, part, dev):
        cols = pl.ds(part * HD, HD)
        made = []
        for i, (own, win) in enumerate(((k_hbm, kw), (v_hbm, vw))):
            src = own.at[:, cols] if src_slot is None else win.at[src_slot, :, cols]
            made.append(
                pltpu.make_async_remote_copy(
                    src_ref=src,
                    dst_ref=win.at[dst_slot, :, cols],
                    send_sem=send_sem.at[kind, part, i],
                    recv_sem=recv_sem.at[dst_slot, part, i],
                    device_id=dev,
                    device_id_type=MESH,
                )
            )
        return made

    def start(*args):
        for copy in copies(*args):
            copy.start()

    def arrived(slot, part):
        for copy in copies(None, slot, 0, part, sibling):
            copy.wait_recv()

    def sent(kind, part):
        for copy in copies(None, 0, kind, part, sibling):
            copy.wait_send()

    first_chip = g < 2
    def launch(part):
        @pl.when(to4)
        def _():
            start(None, 0, 0, part, at(me + 4))

        if relay:

            @pl.when(first_chip)
            def _():
                start(None, 2, 1, part, across)

        else:

            @pl.when(to2)
            def _():
                start(None, 2, 1, part, at(me + 2))

    def settle(part):
        @pl.when(to4)
        def _():
            sent(0, part)

        @pl.when(first_chip if relay else to2)
        def _():
            sent(1, part)

    for part in range(2):
        launch(part)

    @pl.when(core == 0)
    def _():
        for part in range(HK):
            start(None, 3, 2, part, sibling)

    def pass_on_far(part):
        @pl.when(has4)
        def _():
            arrived(0, part)

        if relay:

            @pl.when(jnp.logical_not(first_chip))
            def _():
                start(0, 2, 1, part, across)

        @pl.when(core == 1)
        def _():
            start(0, 1, 2, part, sibling)

    def pass_on_near(part):
        if relay:
            arrived(2, part)
        else:

            @pl.when(has2)
            def _():
                arrived(2, part)

        @pl.when(core == 0)
        def _():
            start(2, 1, 3, part, sibling)

        @pl.when(core == 1)
        def _():
            start(2, 3, 3, part, sibling)

    for copy in small:
        copy.wait()
    first = me * rows
    pos = first + lax.broadcasted_iota(jnp.int32, (rows, HD), 0)

    def doc(j, carry):
        total, begin = carry
        total = total + len_ref[j]
        return total, jnp.where(total <= pos, total, begin)

    _, begin = lax.fori_loop(0, len_ref.shape[0], doc, (jnp.int32(0), jnp.zeros_like(pos)))
    visible = pos - begin + 1
    factor = jnp.log(visible.astype(jnp.float32)) * (math.log2(math.e) / math.sqrt(HD))
    lv[...] = jnp.where(visible == 1, 1.0, factor)
    k_pos = first + lax.broadcasted_iota(jnp.int32, (rows, rows), 1)
    q_pos = first + lax.broadcasted_iota(jnp.int32, (rows, rows), 0)
    seen = (k_pos >= jnp.broadcast_to(begin[:, :1], (rows, rows))) & (k_pos <= q_pos)
    bias[...] = jnp.where(seen, 0.0, MASKED)
    reach[...] = jnp.where(begin < first, 1.0, 0.0)
    w_rows = WIN_DEV * rows
    w_pos = first - w_rows + lax.broadcasted_iota(jnp.int32, (w_rows, HD), 0)
    live[...] = jnp.where(w_pos >= begin[:1], 1.0, 0.0).astype(live.dtype)
    for copy in large:
        copy.wait()

    def head_cols(h):
        return pl.ds(h * HD, HD)

    def scores(q, keys):
        return lax.dot_general(q, keys, (((1,), (1,)), ((), ())), preferred_element_type=jnp.float32)

    def spread(x, width):
        whole = [x] * (width // HD)
        if width % HD:
            whole.append(x[:, : width % HD])
        return jnp.concatenate(whole, axis=1)

    def mix(p, vals):
        return jnp.dot(p.astype(jnp.bfloat16), vals, preferred_element_type=jnp.float32)

    def stacked(t):
        heads = [t * GROUP + j for j in range(GROUP)]
        q = jnp.concatenate([q_ref[:, head_cols(h)] for h in heads], axis=0)
        fac = jnp.concatenate([lv[...] * scale_ref[h] for h in heads], axis=0)
        return q, fac

    def own_part(kv, tiles=range(PER // GROUP)):
        keys = k_ref[:, head_cols(kv)]
        vals = v_ref[:, head_cols(kv)]
        vals = jnp.concatenate([vals, jnp.ones(vals.shape, vals.dtype)], axis=1)
        for i in tiles:
            t = kv * (PER // GROUP) + i
            q, fac = stacked(t)
            s = scores(q, keys).reshape(GROUP, rows, rows) + bias[...][None]
            s = s.reshape(GROUP * rows, rows)
            m = jnp.max(s, axis=1, keepdims=True)
            acc[t] = mix(jnp.exp2((s - m) * spread(fac, rows)), vals)
            top[t] = jnp.broadcast_to(m, top.shape[1:])

    def window_part(kv):
        alive = live[...]
        stand_in = k_ref[:16, head_cols(kv)][:1] * (1 - alive)
        keys = kw[:, :, head_cols(kv)].reshape(w_rows, HD) * alive + stand_in
        vals = vw[:, :, head_cols(kv)].reshape(w_rows, HD) * alive
        vals = jnp.concatenate([vals, alive], axis=1)
        reaching = jnp.concatenate([reach[...]] * GROUP, axis=0)
        reached = reaching > 0
        both_reached = spread(reaching, 2 * HD) > 0
        for i in range(PER // GROUP):
            t = kv * (PER // GROUP) + i
            q, fac = stacked(t)
            s = scores(q, keys)
            m_own = top[t]
            m_win = jnp.broadcast_to(jnp.max(s, axis=1, keepdims=True), m_own.shape)
            m = jnp.where(reached, jnp.maximum(m_own, m_win), m_own)
            mixed = mix(jnp.exp2((s - spread(m, w_rows)) * spread(fac, w_rows)), vals)
            kept = spread(jnp.exp2((m_own - m) * fac), 2 * HD)
            both = acc[t] * kept + jnp.where(both_reached, mixed, 0.0)
            out = (both[:, :HD] / both[:, HD:]).astype(o_ref.dtype)
            for j in range(GROUP):
                o_ref[:, head_cols(t * GROUP + j)] = out[j * rows : (j + 1) * rows]

    own_part(0)
    settle(0)
    launch(2)
    pass_on_far(0)
    own_part(1)
    settle(1)
    launch(3)
    own_part(2)
    pass_on_far(1)
    pass_on_near(0)
    own_part(3)
    pass_on_far(2)
    pass_on_near(1)
    for step in range(HK):
        arrived(1, step)
        arrived(3, step)
        window_part(step)
        if step == 0:
            pass_on_near(2)
            pass_on_far(3)
        if step == 1:
            pass_on_near(3)

    settle(2)
    settle(3)
    if relay:

        @pl.when(jnp.logical_not(first_chip))
        def _():
            for part in range(HK):
                sent(1, part)

    for part in range(HK):
        sent(2, part)
        sent(3, part)


def body(queries, keys, values, lengths, ssmax_scale):
    rows = queries.shape[0]
    n_ctx, n_grp = lax.axis_size("ctx"), lax.axis_size("grp")
    vmem = pl.BlockSpec(memory_space=pltpu.VMEM)
    hbm = pl.BlockSpec(memory_space=pltpu.HBM)
    window = pltpu.VMEM((WIN_DEV, rows, HK * HD), jnp.bfloat16)
    pairs = HQ * rows * (WIN_DEV + 1) * rows
    return pl.pallas_call(
        functools.partial(kernel, n_ctx, n_grp),
        out_shape=jax.ShapeDtypeStruct(queries.shape, queries.dtype),
        in_specs=[hbm] * 5,
        out_specs=vmem,
        scratch_shapes=[
            pltpu.SMEM(ssmax_scale.shape, ssmax_scale.dtype),
            pltpu.SMEM(lengths.shape, lengths.dtype),
            pltpu.VMEM(queries.shape, queries.dtype),
            pltpu.VMEM(keys.shape, keys.dtype),
            pltpu.VMEM(values.shape, values.dtype),
            window,
            window,
            pltpu.VMEM((rows, rows), jnp.float32),
            pltpu.VMEM((rows, HD), jnp.float32),
            pltpu.VMEM((WIN_DEV * rows, HD), jnp.bfloat16),
            pltpu.VMEM((rows, HD), jnp.float32),
            pltpu.VMEM((HQ // GROUP, GROUP * rows, 2 * HD), jnp.float32),
            pltpu.VMEM((HQ // GROUP, GROUP * rows, HD), jnp.float32),
            pltpu.SemaphoreType.DMA((5,)),
            pltpu.SemaphoreType.DMA((4, HK, 2)),
            pltpu.SemaphoreType.DMA((4, HK, 2)),
        ],
        compiler_params=pltpu.CompilerParams(
            collective_id=0, has_side_effects=True, vmem_limit_bytes=48 * 1024 * 1024
        ),
        cost_estimate=pl.CostEstimate(
            flops=4 * pairs * HD, bytes_accessed=4 * queries.size, transcendentals=pairs
        ),
    )(*[pltpu.with_memory_space_constraint(x, pltpu.HBM) for x in (ssmax_scale, lengths, queries, keys, values)])


def solution(mesh):
    spec = P(("ctx", "grp"), None)
    return jax.shard_map(
        body,
        mesh=mesh,
        in_specs=(spec, spec, spec, P(), P()),
        out_specs=spec,
        check_vma=False,
    )
```
